32 devices in a mesh: grp: 2 (over y), ep: 8 (over z, core), tp: 2 (over x).
Axes of the slice: x: 2, y: 2, z: 4, core: 2. Of those that a mesh axis runs over, the one named last changes fastest.
Arguments:
- queries: bfloat16 [1024, 8192], P(('grp', 'ep'), 'tp'), parts along dimension 0, may hold values from -6 to 6
- draft_kv: bfloat16 [1024, 512], P(('grp', 'ep')), parts along dimension 0, may hold values from -6 to 6
- kv_cache: bfloat16 [256, 256, 512], P(('grp', 'ep', 'tp')), parts along dimension 0, may hold values from -6 to 6
- lengths: int32 [256], P(('grp', 'ep')), parts along dimension 0, may hold values from 1 to 256, as said below
- residual: bfloat16 [1024, 3584], P(('grp', 'ep', 'tp')), parts along dimension 0, may hold values from -6 to 6
- out_proj: bfloat16 [8192, 3584], P('tp'), may hold values from -0.5 to 0.5
- norm_gain: float32 [3584], replicated, may hold values from 0.1 to 1.9
- up_proj: bfloat16 [8, 3584, 2560], P('ep', None, 'tp'), may hold values from -0.09375 to 0.09375
- down_proj: bfloat16 [8, 2560, 3584], P('ep', 'tp'), may hold values from -0.125 to 0.125
- routes: int32 [1024, 3], P(('grp', 'ep', 'tp')), parts along dimension 0, may hold values from 0 to 7, all different within a row; in each aligned block of 32 rows (0 to 31, 32 to 63, ...) at most 12 rows name the same one
- route_gates: float32 [1024, 3], P(('grp', 'ep', 'tp')), parts along dimension 0, may hold values from 0.2 to 1
- lost_device: int32 [2], P('grp'), parts along dimension 0, may hold values from 0 to 7
- spare_table: int32 [16], P('grp'), parts along dimension 0, may hold values from 0 to 7, as said below
Outputs:
- layer_out: bfloat16 [1024, 3584], P(('grp', 'ep', 'tp')), parts along dimension 0
The draws below stay inside these ranges and needn't reach their ends.
There are 2 independent parts, one for each index of `grp`. The reference program is written for one: setup_inputs(seed, part) draws one part's arguments, and reference() takes and returns one part's arrays. A program takes and returns all parts, laid end to end along the dimension named above; an argument that names none is the same for every part. Nothing has to cross between parts.
Inputs may be any that keep to these rules, and one draw needn't show every extreme that they name: lengths reach 256 in every draw. `routes`: each row names 3 different experts; in the rows of one device (aligned blocks of 32 rows) no expert is named by more than 12 rows. `spare_table`: no entry equals its own index.
All inputs are finite; a program needn't handle non-finite values.
Results may differ from the reference program's by a relative error of at most 0.013.
Values may be sent and summed in bfloat16 or wider, within the bound.
A program may use at most 192 MiB of HBM per device.

```python
import math
import jax
import jax.numpy as jnp
import numpy as np
from jax import lax

D = 3584
FF = 2560
HEADS = 32
HD = 256
DRAFT = 4
TOPK = 3
CACHE = 256
REQUESTS = 128
ROWS = 512
TP_ROWS = 32
EXPERTS = 8
CAP = 12
N_TP = 2


def draw_queries(key, part):
    key = jax.random.fold_in(key, 11)
    values = jnp.clip(jax.random.normal(key, (ROWS, HEADS, HD), jnp.float32), -6.0, 6.0)
    return values.reshape(ROWS, HEADS * HD).astype(jnp.bfloat16)


def draw_draft_kv(key, part):
    key = jax.random.fold_in(key, 23)
    values = jnp.clip(jax.random.normal(key, (ROWS, 2 * HD), jnp.float32), -6.0, 6.0)
    return values.astype(jnp.bfloat16)


def draw_kv_cache(key, part):
    key = jax.random.fold_in(key, 31)
    values = jnp.clip(jax.random.normal(key, (REQUESTS, CACHE, 2 * HD), jnp.float32), -6.0, 6.0)
    return values.astype(jnp.bfloat16)


def draw_lengths(key, part):
    key = jax.random.fold_in(key, 41)
    values = jax.random.randint(key, (REQUESTS,), 1, CACHE + 1)
    return values.at[0].set(CACHE).astype(jnp.int32)


def draw_spare_table(key, part):
    key = jax.random.fold_in(key, 53)
    offset = jax.random.randint(key, (EXPERTS,), 1, EXPERTS)
    return ((jnp.arange(EXPERTS) + offset) % EXPERTS).astype(jnp.int32)


def block_scale(rng, extent, split, least, top_value):
    def one(axis_at, shards_of):
        draws = jax.random.uniform(jax.random.fold_in(jax.random.fold_in(rng, 6), axis_at), (shards_of,), jnp.float32, least / len(split), top_value / len(split))
        return jnp.repeat(jnp.exp(draws), extent[axis_at] // shards_of).reshape((-1,) + (1,) * (len(extent) - axis_at - 1))

    loudness = one(*split[0])
    for cut in split[1:]:
        loudness = loudness * one(*cut)
    return loudness


def deal_out(rng, own, number, rows, count, top, limit, lean):
    order = jax.random.permutation(rng, count)
    crowded, ordinary = shares(count, rows * top, limit, lean, True), shares(count, rows * top, limit, lean, False)
    places = jnp.arange(count)

    def named(tallies, rotation):
        used = int((tallies > 0).sum())
        fixed = max(1, used // 4)
        shifted = fixed + (places - fixed + rotation * (used - fixed)) % max(1, count - fixed)
        return jnp.zeros((count,), jnp.int32).at[order[jnp.where(places < fixed, places, shifted)]].set(jnp.asarray(tallies, jnp.int32))

    tallies = jnp.where(number % 4 == 0, named(crowded, number // 4), named(ordinary, number - number // 4 - 1))
    mixed = jax.random.permutation(jax.random.fold_in(own, 3), count)
    giver, taker = mixed[0:count // 2 * 2:2], mixed[1:count // 2 * 2:2]
    slack = jnp.minimum(tallies[giver] - 1, limit - tallies[taker]) // 2
    slack = jnp.where((giver == order[0]) | (taker == order[0]) | (tallies[taker] == 0), 0, jnp.maximum(slack, 0))
    shifted = jax.random.randint(jax.random.fold_in(own, 4), (count // 2,), 0, 1 << 20) % (slack + 1)
    tallies = tallies.at[giver].add(-shifted).at[taker].add(shifted)
    items = jnp.searchsorted(jnp.cumsum(tallies), jnp.arange(rows * top), side="right").astype(jnp.int32)
    table = items.reshape(top, rows).T
    table = table[jax.random.permutation(jax.random.fold_in(own, 1), rows)]
    rotation = jax.random.randint(jax.random.fold_in(own, 2), (rows, 1), 0, top)
    return jnp.take_along_axis(table, (jnp.arange(top)[None, :] + rotation) % top, axis=1)


def shares(count, total, most, lean, full):
    weights = [(1 << 20) // math.isqrt(standing ** lean) + 1 for standing in range(1, count + 1)]
    largest = most if full else min(most, max(-(-total // count), total * weights[0] // sum(weights)))
    least = 1 if total - largest >= count - 1 else 0
    holding, surplus = [largest] + [least] * (count - 1), total - largest - least * (count - 1)
    while surplus > 0:
        candidates = [i for i in range(1, count) if holding[i] < largest] or [i for i in range(1, count) if holding[i] < most]
        mass, remaining = sum([weights[i] for i in candidates]), surplus
        for i in candidates:
            more = min(most - holding[i], max(1, remaining * weights[i] // mass), surplus)
            holding[i] = holding[i] + more
            surplus = surplus - more
    return np.array(holding)


def centred(own_key, dims, width, bound, shards=(), dtype=jnp.bfloat16):
    drawn = jax.random.normal(own_key, dims, jnp.float32) * width
    if len(shards) > 0:
        drawn = block_scale(own_key, dims, shards, -0.22, 0.18) * drawn
    return jnp.clip(drawn, min=-bound, max=bound).astype(dtype)


def setup_inputs(seed: int = 0, part: int = 0) -> dict:
    splits = jax.random.split(jax.random.key(seed), 14)
    part_splits = jax.random.split(jax.random.fold_in(splits[13], part), 14)
    queries = draw_queries(jax.random.fold_in(jax.random.fold_in(splits[13], part), 71), part)
    draft_kv = draw_draft_kv(jax.random.fold_in(jax.random.fold_in(splits[13], part), 71), part)
    kv_cache = draw_kv_cache(jax.random.fold_in(jax.random.fold_in(splits[13], part), 71), part)
    lengths = draw_lengths(jax.random.fold_in(jax.random.fold_in(splits[13], part), 71), part)
    residual = centred(part_splits[4], (ROWS, D), 1.0, 6.0, ((0, 16),))
    out_proj = centred(splits[5], (HEADS * HD, D), (HD // 2) ** -0.5, 0.5, ((0, 2),))
    norm_gain = jnp.clip(1.0 + 0.18 * jax.random.normal(splits[6], (D,), jnp.float32), 0.1, 1.9)
    up_proj = centred(splits[7], (EXPERTS, D, FF), D ** -0.5, 0.09375, ((0, 8), (2, 2)))
    down_proj = centred(splits[8], (EXPERTS, FF, D), FF ** -0.5, 0.125, ((0, 8), (1, 2)))
    routes_keys = jax.random.split(jax.random.fold_in(part_splits[9], 1), ROWS // TP_ROWS)
    routes_turns = jax.random.permutation(jax.random.fold_in(part_splits[9], 3), ROWS // TP_ROWS)
    routes = jax.vmap(lambda own, number: deal_out(jax.random.fold_in(part_splits[9], 2), own, number, TP_ROWS, EXPERTS, TOPK, CAP, 0))(routes_keys, routes_turns).reshape((ROWS, TOPK))
    route_gates = jnp.clip(0.2 + 0.8 * jax.random.uniform(part_splits[10], (ROWS, TOPK), jnp.float32) ** block_scale(part_splits[10], (ROWS, TOPK), ((0, 16),), -0.2, 0.2), 0.2, 1.0)
    lost_device = jax.random.randint(part_splits[11], (1,), 0, EXPERTS).astype(jnp.int32)
    spare_table = draw_spare_table(jax.random.fold_in(jax.random.fold_in(splits[13], part), 71), part)
    return dict(queries=queries, draft_kv=draft_kv, kv_cache=kv_cache, lengths=lengths, residual=residual, out_proj=out_proj, norm_gain=norm_gain, up_proj=up_proj, down_proj=down_proj, routes=routes, route_gates=route_gates, lost_device=lost_device, spare_table=spare_table)


EPSILON = 1e-06

def attend_request(packed):
    query_rows, draft_rows, cache_rows, length = packed
    key_rows = jnp.concatenate([cache_rows[:, :HD], draft_rows[:, :HD]], 0).astype(jnp.float32)
    value_rows = jnp.concatenate([cache_rows[:, HD:], draft_rows[:, HD:]], 0).astype(jnp.float32)
    query_heads = query_rows.reshape(DRAFT, HEADS, HD).astype(jnp.float32)
    factor = 1.0 / math.sqrt(HD)
    scores = jnp.einsum('thd,kd->thk', query_heads, key_rows) * factor
    position = jnp.arange(CACHE + DRAFT)
    draft_order = jnp.arange(DRAFT)
    visible = jnp.where(position[None, :] < CACHE, position[None, :] < length, position[None, :] - CACHE <= draft_order[:, None])
    visible = visible[:, None, :]
    peak = lax.optimization_barrier(jnp.max(jnp.where(visible, scores, -jnp.inf), axis=-1, keepdims=True))
    weights = jnp.where(visible, jnp.exp(scores - peak), 0.0)
    totals = lax.optimization_barrier(jnp.sum(weights, axis=-1, keepdims=True))
    rounded = lax.optimization_barrier(weights.astype(jnp.bfloat16)).astype(jnp.float32)
    mixture = jnp.einsum('thk,kd->thd', rounded, value_rows) / totals
    return mixture.reshape(DRAFT, HEADS * HD).astype(jnp.bfloat16)

def reference(queries, draft_kv, kv_cache, lengths, residual, out_proj, norm_gain, up_proj, down_proj, routes, route_gates, lost_device, spare_table):
    attended = lax.map(attend_request, (queries.reshape(REQUESTS, DRAFT, HEADS * HD), draft_kv.reshape(REQUESTS, DRAFT, 2 * HD), kv_cache, lengths))
    attended = attended.reshape(ROWS, HEADS * HD)
    hidden = (residual.astype(jnp.float32) + jnp.dot(attended, out_proj, preferred_element_type=jnp.float32)).astype(jnp.bfloat16)
    widened = hidden.astype(jnp.float32)
    normed = (widened * lax.rsqrt(lax.optimization_barrier(jnp.mean(widened * widened, axis=-1, keepdims=True)) + EPSILON) * norm_gain).astype(jnp.bfloat16)
    lost_id = lost_device[0]
    target = jnp.where(routes == lost_id, spare_table[lost_id], routes).astype(jnp.int32)

    def per_expert(accumulated, expert):
        inner_act = jnp.dot(normed, up_proj[expert], preferred_element_type=jnp.float32)
        active = jax.nn.silu(inner_act).astype(jnp.bfloat16)
        blocks = active.reshape(ROWS, N_TP, FF // N_TP).astype(jnp.float32)
        down_blocks = down_proj[expert].reshape(N_TP, FF // N_TP, D).astype(jnp.float32)
        pieces = jnp.einsum('rjf,jfd->jrd', blocks, down_blocks)
        pieces = lax.optimization_barrier(pieces.astype(jnp.bfloat16)).astype(jnp.float32)
        expert_out = lax.optimization_barrier(jnp.sum(pieces, axis=0))
        weight = lax.optimization_barrier(jnp.sum(jnp.where(target == expert, route_gates, 0.0), axis=-1))
        return (accumulated + weight[:, None] * expert_out, None)
    accumulated, unused = lax.scan(per_expert, jnp.zeros((ROWS, D), jnp.float32), jnp.arange(EXPERTS))
    return (widened + accumulated).astype(jnp.bfloat16)
```

```python
import functools
import math

import jax
import jax.numpy as jnp
from jax import lax
from jax.experimental import pallas as pl
from jax.experimental.pallas import tpu as pltpu
from jax.sharding import PartitionSpec as P

MESH = pl.DeviceIdType.MESH
TILE = 512

EPSILON = 1e-06


def attend_block(q_ref, out_ref, kv, draft, draft_at, lengths, first, head_dim, drafts):
    requests, cached, _ = kv.shape
    heads = q_ref.shape[1] // head_dim
    factor = 1.0 / math.sqrt(head_dim)
    pair = 2 * drafts
    rows = heads * pair
    spread = q_ref[...].astype(jnp.float32)
    draft_keys = draft[draft_at, :, :head_dim]
    draft_values = draft[draft_at, :, head_dim:]
    mixed = []
    for p in range(requests // 2):
        here = jnp.concatenate(
            [
                spread[p * pair : (p + 1) * pair, h * head_dim : (h + 1) * head_dim]
                for h in range(heads)
            ],
            0,
        ).astype(jnp.bfloat16)
        keys = kv[2 * p : 2 * p + 2, :, :head_dim].reshape(2 * cached, head_dim)
        values = kv[2 * p : 2 * p + 2, :, head_dim:].reshape(2 * cached, head_dim)
        scores = (
            lax.dot_general(
                here, keys, (((1,), (1,)), ((), ())), preferred_element_type=jnp.float32
            )
            * factor
        )
        row = lax.broadcasted_iota(jnp.int32, scores.shape, 0) % pair
        column = lax.broadcasted_iota(jnp.int32, scores.shape, 1)
        upper = row >= drafts
        length = jnp.where(upper, lengths[first + 2 * p + 1] + cached, lengths[first + 2 * p])
        begin = jnp.where(upper, cached, 0)
        seen = (column >= begin) & (column < length)
        late = (
            lax.dot_general(
                here, draft_keys, (((1,), (1,)), ((), ())), preferred_element_type=jnp.float32
            )
            * factor
        )
        late_row = lax.broadcasted_iota(jnp.int32, late.shape, 0) % pair
        late_column = lax.broadcasted_iota(jnp.int32, late.shape, 1)
        late_begin = jnp.where(late_row >= drafts, drafts, 0) + p * pair
        late_seen = (late_column >= late_begin) & (late_column <= late_row + p * pair)
        scores = jnp.where(seen, scores, -jnp.inf)
        late = jnp.where(late_seen, late, -jnp.inf)
        peak = jnp.maximum(
            jnp.max(scores, axis=1, keepdims=True), jnp.max(late, axis=1, keepdims=True)
        )
        weights = jnp.exp(scores - peak)
        late_weights = jnp.exp(late - peak)
        totals = jnp.sum(weights, axis=1, keepdims=True) + jnp.sum(
            late_weights, axis=1, keepdims=True
        )
        mixture = jnp.dot(
            weights.astype(jnp.bfloat16), values, preferred_element_type=jnp.float32
        ) + jnp.dot(
            late_weights.astype(jnp.bfloat16), draft_values, preferred_element_type=jnp.float32
        )
        mixed.append(mixture / totals)
    for h in range(heads):
        out_ref[:, h * head_dim : (h + 1) * head_dim] = jnp.concatenate(
            [part[h * pair : (h + 1) * pair] for part in mixed], 0
        ).astype(jnp.bfloat16)


def attend_kernel(
    q,
    draft,
    kv,
    lengths,
    residual,
    w,
    gain,
    hidden_out,
    normed_out,
    q_own,
    q_in,
    kv_v,
    w_v,
    att_own,
    att_out,
    att_in,
    total,
    proj_out,
    proj_in,
    local_sem,
    w_sem,
    q_sem,
    att_sem,
    send_sem,
    recv_sem,
):
    me = lax.axis_index("tp")
    peer = 1 - me
    head_dim = kv.shape[2] // 2
    requests = kv.shape[0]
    drafts = q.shape[1] // requests
    tiles = w_v.shape[0]
    q_copy = pltpu.make_async_copy(q.at[me], q_own, local_sem.at[0])
    kv_copy = pltpu.make_async_copy(kv, kv_v, local_sem.at[1])
    q_copy.start()
    kv_copy.start()

    def w_copy(n):
        return pltpu.make_async_copy(
            w.at[:, pl.ds(pl.multiple_of(n * TILE, TILE), TILE)], w_v.at[n], w_sem.at[n]
        )

    for n in range(tiles):
        w_copy(n).start()
    barrier = pltpu.get_barrier_semaphore()
    pl.semaphore_signal(barrier, inc=1, device_id={"tp": peer}, device_id_type=MESH)
    pl.semaphore_wait(barrier, 1)

    def remote(source, target, send, recv):
        return pltpu.make_async_remote_copy(
            src_ref=source,
            dst_ref=target,
            send_sem=send,
            recv_sem=recv,
            device_id={"tp": peer},
            device_id_type=MESH,
        )

    ask = remote(q.at[peer], q_in, q_sem.at[0], q_sem.at[1])
    ask.start()
    q_copy.wait()
    kv_copy.wait()
    first = me * requests
    attend_block(q_own, att_own, kv_v, draft, me, lengths, first, head_dim, drafts)
    ask.wait()
    attend_block(q_in, att_out, kv_v, draft, me, lengths, first, head_dim, drafts)
    answer = remote(att_out, att_in, att_sem.at[0], att_sem.at[1])
    answer.start()

    def own_part(n, carry):
        w_copy(n).wait()
        total[n] = jnp.dot(att_own[...], w_v[n], preferred_element_type=jnp.float32)
        return carry

    lax.fori_loop(0, tiles, own_part, 0)
    answer.wait()

    def give(n):
        return remote(proj_out.at[n], proj_in.at[n], send_sem.at[n], recv_sem.at[n])

    def peer_part(n, carry):
        proj_out[n] = jnp.dot(
            att_in[...], w_v[n], preferred_element_type=jnp.float32
        ).astype(jnp.bfloat16)
        give(n).start()
        return carry

    lax.fori_loop(0, tiles, peer_part, 0)
    squares = jnp.zeros((residual.shape[0], 1), jnp.float32)
    for n in range(tiles):
        give(n).wait()
        lanes = slice(n * TILE, (n + 1) * TILE)
        hidden = (
            residual[:, lanes].astype(jnp.float32)
            + total[n]
            + proj_in[n].astype(jnp.float32)
        ).astype(jnp.bfloat16)
        hidden_out[:, lanes] = hidden
        widened = hidden.astype(jnp.float32)
        squares += jnp.sum(widened * widened, axis=1, keepdims=True)
    scale = lax.rsqrt(squares / residual.shape[1] + EPSILON)
    for n in range(tiles):
        lanes = slice(n * TILE, (n + 1) * TILE)
        normed_out[:, lanes] = (
            hidden_out[:, lanes].astype(jnp.float32) * scale * gain[:, lanes]
        ).astype(jnp.bfloat16)


def attend_paired(queries, draft_kv, kv_cache, lengths, residual, out_proj, norm_gain):
    rows, features = residual.shape
    width = queries.shape[1]
    tiles = features // TILE
    vmem = pl.BlockSpec(memory_space=pltpu.VMEM)
    hbm = pl.BlockSpec(memory_space=pl.ANY)
    half = jax.ShapeDtypeStruct((rows, features), jnp.bfloat16)
    return pl.pallas_call(
        attend_kernel,
        out_shape=(half, half),
        in_specs=[
            hbm,
            vmem,
            hbm,
            pl.BlockSpec(memory_space=pltpu.SMEM),
            vmem,
            hbm,
            vmem,
        ],
        out_specs=(vmem, vmem),
        scratch_shapes=[
            pltpu.VMEM((rows, width), jnp.bfloat16),
            pltpu.VMEM((rows, width), jnp.bfloat16),
            pltpu.VMEM(kv_cache.shape, jnp.bfloat16),
            pltpu.VMEM((tiles, width, TILE), jnp.bfloat16),
            pltpu.VMEM((rows, width), jnp.bfloat16),
            pltpu.VMEM((rows, width), jnp.bfloat16),
            pltpu.VMEM((rows, width), jnp.bfloat16),
            pltpu.VMEM((tiles, rows, TILE), jnp.float32),
            pltpu.VMEM((tiles, rows, TILE), jnp.bfloat16),
            pltpu.VMEM((tiles, rows, TILE), jnp.bfloat16),
            pltpu.SemaphoreType.DMA((2,)),
            pltpu.SemaphoreType.DMA((tiles,)),
            pltpu.SemaphoreType.DMA((2,)),
            pltpu.SemaphoreType.DMA((2,)),
            pltpu.SemaphoreType.DMA((tiles,)),
            pltpu.SemaphoreType.DMA((tiles,)),
        ],
        compiler_params=pltpu.CompilerParams(
            collective_id=0, has_side_effects=True, vmem_limit_bytes=48 * 1024 * 1024
        ),
    )(
        queries.reshape(2, rows, width),
        draft_kv.reshape(2, rows, draft_kv.shape[1]),
        kv_cache,
        lengths,
        residual,
        out_proj,
        norm_gain.reshape(1, features),
    )


def attend_general(queries, draft_kv, kv_cache, lengths, residual, out_proj, norm_gain):
    requests = lengths.shape[0]
    drafts = draft_kv.shape[0] // requests
    head_dim = draft_kv.shape[1] // 2
    head_count = queries.shape[1] // head_dim
    factor = 1.0 / math.sqrt(head_dim)
    query_heads = queries.reshape(requests, drafts, head_count, head_dim)
    draft_rows = draft_kv.reshape(requests, drafts, 2 * head_dim)
    draft_order = jnp.arange(drafts)
    block_rows = lax.all_gather(kv_cache, "tp", axis=0, tiled=True)
    amount = block_rows.shape[0]
    cached = block_rows.shape[1]
    key_rows = jnp.concatenate([block_rows[:, :, :head_dim], draft_rows[:, :, :head_dim]], 1)
    value_rows = jnp.concatenate([block_rows[:, :, head_dim:], draft_rows[:, :, head_dim:]], 1)
    scores = (
        jnp.einsum("rthd,rkd->rthk", query_heads, key_rows, preferred_element_type=jnp.float32)
        * factor
    )
    position = jnp.arange(cached + drafts)
    visible = jnp.where(
        position[None, None, :] < cached,
        position[None, None, :] < lengths[:, None, None],
        position[None, None, :] - cached <= draft_order[None, :, None],
    )
    visible = visible[:, :, None, :]
    peak = jnp.max(jnp.where(visible, scores, -jnp.inf), axis=-1, keepdims=True)
    weights = jnp.where(visible, jnp.exp(scores - peak), 0.0)
    totals = jnp.sum(weights, axis=-1, keepdims=True)
    mixture = (
        jnp.einsum(
            "rthk,rkd->rthd",
            weights.astype(jnp.bfloat16),
            value_rows,
            preferred_element_type=jnp.float32,
        )
        / totals
    )
    attended = mixture.astype(jnp.bfloat16).reshape(amount * drafts, head_count * head_dim)
    kept_rows = residual.shape[0]
    features = residual.shape[1]
    summed = lax.psum_scatter(
        jnp.dot(attended, out_proj, preferred_element_type=jnp.float32).astype(jnp.bfloat16),
        "tp",
        scatter_dimension=0,
        tiled=True,
    ).astype(jnp.float32)
    hidden = (residual.astype(jnp.float32) + summed).astype(jnp.bfloat16)
    widened = hidden.astype(jnp.float32)
    normed = (
        widened
        * lax.rsqrt(jnp.mean(widened * widened, axis=-1, keepdims=True) + EPSILON)
        * norm_gain
    ).astype(jnp.bfloat16)
    return hidden, normed


def shards(
    queries,
    draft_kv,
    kv_cache,
    lengths,
    residual,
    out_proj,
    norm_gain,
    up_proj,
    down_proj,
    routes,
    route_gates,
    lost_device,
    spare_table,
):
    kept_rows, features = residual.shape
    paired = lax.axis_size("tp") == 2 and kv_cache.shape[0] % 8 == 0
    attend = attend_paired if paired else attend_general
    hidden, normed = attend(
        queries, draft_kv, kv_cache, lengths, residual, out_proj, norm_gain
    )
    widened = hidden.astype(jnp.float32)
    experts = lax.axis_size("ep")
    tp_lanes = lax.axis_size("tp")
    per_row = routes.shape[1]
    capacity = min(kept_rows, (kept_rows * per_row + experts - 1) // experts)
    lost_id = lost_device[0]
    spare_id = jnp.sum(jnp.where(jnp.arange(experts) == lost_id, spare_table, 0))
    flat_routes = routes.reshape(-1)
    is_lost = flat_routes == lost_id
    lost_count = is_lost.astype(jnp.int32)
    earlier_lost = jnp.cumsum(lost_count) - lost_count
    one_hot = (flat_routes[:, None] == jnp.arange(experts)[None, :]).astype(jnp.int32)
    earlier_same = jnp.sum((jnp.cumsum(one_hot, axis=0) - one_hot) * one_hot, axis=1)
    slot_count = 2 * capacity
    target = jnp.where(is_lost, spare_id, flat_routes)
    slot_place = jnp.where(is_lost, capacity + earlier_lost, earlier_same)
    spare_up, spare_down = (up_proj, down_proj)
    slot_index = target * slot_count + slot_place
    selector = (slot_index[None, :] == jnp.arange(experts * slot_count)[:, None]).astype(
        jnp.bfloat16
    )
    repeated = jnp.repeat(normed, per_row, axis=0)
    outgoing = jnp.dot(selector, repeated, preferred_element_type=jnp.float32).astype(jnp.bfloat16)
    outgoing = outgoing.reshape(experts, slot_count, features)
    copies = jnp.broadcast_to(outgoing[:, None], (experts, tp_lanes, slot_count, features))
    copies = copies.reshape(experts * tp_lanes, slot_count, features)
    arrived = lax.all_to_all(copies, ("ep", "tp"), split_axis=0, concat_axis=0, tiled=True)
    main_part = jnp.einsum(
        "nsd,df->nsf", arrived[:, :capacity], up_proj[0], preferred_element_type=jnp.float32
    )
    spare_part = jnp.einsum(
        "nsd,df->nsf", arrived[:, capacity:], spare_up[0], preferred_element_type=jnp.float32
    )
    main_out = jnp.einsum(
        "nsf,fd->nsd",
        jax.nn.silu(main_part).astype(jnp.bfloat16),
        down_proj[0],
        preferred_element_type=jnp.float32,
    )
    spare_out = jnp.einsum(
        "nsf,fd->nsd",
        jax.nn.silu(spare_part).astype(jnp.bfloat16),
        spare_down[0],
        preferred_element_type=jnp.float32,
    )
    terms = jnp.concatenate([main_out, spare_out], axis=1).astype(jnp.bfloat16)
    returned_parts = lax.all_to_all(terms, ("ep", "tp"), split_axis=0, concat_axis=0, tiled=True)
    returned = jnp.sum(
        returned_parts.reshape(experts, tp_lanes, slot_count, features).astype(jnp.float32), axis=1
    )
    slot_grid = slot_index.reshape(kept_rows, per_row)
    combine = jnp.sum(
        jnp.where(
            slot_grid[:, :, None] == jnp.arange(experts * slot_count)[None, None, :],
            route_gates[:, :, None],
            0.0,
        ),
        axis=1,
    )
    expert_sum = jnp.dot(
        combine,
        returned.reshape(experts * slot_count, features),
        precision=lax.Precision.HIGHEST,
        preferred_element_type=jnp.float32,
    )
    return (widened + expert_sum).astype(jnp.bfloat16)


def solution(mesh):
    return jax.shard_map(
        shards,
        mesh=mesh,
        in_specs=(
            P(("grp", "ep"), "tp"),
            P(("grp", "ep"), None),
            P(("grp", "ep", "tp"), None, None),
            P(("grp", "ep")),
            P(("grp", "ep", "tp"), None),
            P("tp", None),
            P(),
            P("ep", None, "tp"),
            P("ep", "tp", None),
            P(("grp", "ep", "tp"), None),
            P(("grp", "ep", "tp"), None),
            P("grp"),
            P("grp"),
        ),
        out_specs=P(("grp", "ep", "tp"), None),
        check_vma=False,
    )
```

```python
import functools
import math

import jax
import jax.numpy as jnp
from jax import lax
from jax.experimental import pallas as pl
from jax.experimental.pallas import tpu as pltpu
from jax.sharding import PartitionSpec as P

MESH = pl.DeviceIdType.MESH
TILE = 512

EPSILON = 1e-06


def attend_block(q_ref, out_ref, kv, draft, draft_at, lengths, first, head_dim, drafts):
    requests, cached, _ = kv.shape
    heads = q_ref.shape[1] // head_dim
    factor = 1.0 / math.sqrt(head_dim)
    pair = 2 * drafts
    rows = heads * pair
    spread = q_ref[...].astype(jnp.float32)
    draft_keys = draft[draft_at, :, :head_dim]
    draft_values = draft[draft_at, :, head_dim:]
    mixed = []
    for p in range(requests // 2):
        here = jnp.concatenate(
            [
                spread[p * pair : (p + 1) * pair, h * head_dim : (h + 1) * head_dim]
                for h in range(heads)
            ],
            0,
        ).astype(jnp.bfloat16)
        keys = kv[2 * p : 2 * p + 2, :, :head_dim].reshape(2 * cached, head_dim)
        values = kv[2 * p : 2 * p + 2, :, head_dim:].reshape(2 * cached, head_dim)
        scores = (
            lax.dot_general(
                here, keys, (((1,), (1,)), ((), ())), preferred_element_type=jnp.float32
            )
            * factor
        )
        row = lax.broadcasted_iota(jnp.int32, scores.shape, 0) % pair
        column = lax.broadcasted_iota(jnp.int32, scores.shape, 1)
        upper = row >= drafts
        length = jnp.where(upper, lengths[first + 2 * p + 1] + cached, lengths[first + 2 * p])
        begin = jnp.where(upper, cached, 0)
        seen = (column >= begin) & (column < length)
        late = (
            lax.dot_general(
                here, draft_keys, (((1,), (1,)), ((), ())), preferred_element_type=jnp.float32
            )
            * factor
        )
        late_row = lax.broadcasted_iota(jnp.int32, late.shape, 0) % pair
        late_column = lax.broadcasted_iota(jnp.int32, late.shape, 1)
        late_begin = jnp.where(late_row >= drafts, drafts, 0) + p * pair
        late_seen = (late_column >= late_begin) & (late_column <= late_row + p * pair)
        scores = jnp.where(seen, scores, -jnp.inf)
        late = jnp.where(late_seen, late, -jnp.inf)
        peak = jnp.maximum(
            jnp.max(scores, axis=1, keepdims=True), jnp.max(late, axis=1, keepdims=True)
        )
        weights = jnp.exp(scores - peak)
        late_weights = jnp.exp(late - peak)
        totals = jnp.sum(weights, axis=1, keepdims=True) + jnp.sum(
            late_weights, axis=1, keepdims=True
        )
        mixture = jnp.dot(
            weights.astype(jnp.bfloat16), values, preferred_element_type=jnp.float32
        ) + jnp.dot(
            late_weights.astype(jnp.bfloat16), draft_values, preferred_element_type=jnp.float32
        )
        mixed.append(mixture / totals)
    for h in range(heads):
        out_ref[:, h * head_dim : (h + 1) * head_dim] = jnp.concatenate(
            [part[h * pair : (h + 1) * pair] for part in mixed], 0
        ).astype(jnp.bfloat16)


def attend_kernel(
    q,
    draft,
    kv,
    lengths,
    residual,
    w,
    gain,
    hidden_out,
    normed_out,
    q_own,
    q_in,
    kv_v,
    w_v,
    att_own,
    att_out,
    att_in,
    total,
    proj_out,
    proj_in,
    local_sem,
    w_sem,
    q_sem,
    att_sem,
    send_sem,
    recv_sem,
):
    me = lax.axis_index("tp")
    peer = 1 - me
    head_dim = kv.shape[2] // 2
    requests = kv.shape[0]
    drafts = q.shape[1] // requests
    tiles = w_v.shape[0]
    q_copy = pltpu.make_async_copy(q.at[me], q_own, local_sem.at[0])
    kv_copy = pltpu.make_async_copy(kv, kv_v, local_sem.at[1])
    q_copy.start()
    kv_copy.start()

    def w_copy(n):
        return pltpu.make_async_copy(
            w.at[:, pl.ds(pl.multiple_of(n * TILE, TILE), TILE)], w_v.at[n], w_sem.at[n]
        )

    for n in range(tiles):
        w_copy(n).start()
    barrier = pltpu.get_barrier_semaphore()
    pl.semaphore_signal(barrier, inc=1, device_id={"tp": peer}, device_id_type=MESH)
    pl.semaphore_wait(barrier, 1)

    def remote(source, target, send, recv):
        return pltpu.make_async_remote_copy(
            src_ref=source,
            dst_ref=target,
            send_sem=send,
            recv_sem=recv,
            device_id={"tp": peer},
            device_id_type=MESH,
        )

    ask = remote(q.at[peer], q_in, q_sem.at[0], q_sem.at[1])
    ask.start()
    q_copy.wait()
    kv_copy.wait()
    first = me * requests
    attend_block(q_own, att_own, kv_v, draft, me, lengths, first, head_dim, drafts)
    ask.wait()
    attend_block(q_in, att_out, kv_v, draft, me, lengths, first, head_dim, drafts)
    answer = remote(att_out, att_in, att_sem.at[0], att_sem.at[1])
    answer.start()

    def own_part(n, carry):
        w_copy(n).wait()
        total[n] = jnp.dot(att_own[...], w_v[n], preferred_element_type=jnp.float32)
        return carry

    lax.fori_loop(0, tiles, own_part, 0)
    answer.wait()

    def give(n):
        return remote(proj_out.at[n], proj_in.at[n], send_sem.at[n], recv_sem.at[n])

    def peer_part(n, carry):
        proj_out[n] = jnp.dot(
            att_in[...], w_v[n], preferred_element_type=jnp.float32
        ).astype(jnp.bfloat16)
        give(n).start()
        return carry

    lax.fori_loop(0, tiles, peer_part, 0)
    squares = jnp.zeros((residual.shape[0], 1), jnp.float32)
    for n in range(tiles):
        give(n).wait()
        lanes = slice(n * TILE, (n + 1) * TILE)
        hidden = (
            residual[:, lanes].astype(jnp.float32)
            + total[n]
            + proj_in[n].astype(jnp.float32)
        ).astype(jnp.bfloat16)
        hidden_out[:, lanes] = hidden
        widened = hidden.astype(jnp.float32)
        squares += jnp.sum(widened * widened, axis=1, keepdims=True)
    scale = lax.rsqrt(squares / residual.shape[1] + EPSILON)
    for n in range(tiles):
        lanes = slice(n * TILE, (n + 1) * TILE)
        normed_out[:, lanes] = (
            hidden_out[:, lanes].astype(jnp.float32) * scale * gain[:, lanes]
        ).astype(jnp.bfloat16)


def attend_paired(queries, draft_kv, kv_cache, lengths, residual, out_proj, norm_gain):
    rows, features = residual.shape
    width = queries.shape[1]
    tiles = features // TILE
    vmem = pl.BlockSpec(memory_space=pltpu.VMEM)
    hbm = pl.BlockSpec(memory_space=pl.ANY)
    half = jax.ShapeDtypeStruct((rows, features), jnp.bfloat16)
    return pl.pallas_call(
        attend_kernel,
        out_shape=(half, half),
        in_specs=[
            hbm,
            vmem,
            hbm,
            pl.BlockSpec(memory_space=pltpu.SMEM),
            vmem,
            hbm,
            vmem,
        ],
        out_specs=(vmem, vmem),
        scratch_shapes=[
            pltpu.VMEM((rows, width), jnp.bfloat16),
            pltpu.VMEM((rows, width), jnp.bfloat16),
            pltpu.VMEM(kv_cache.shape, jnp.bfloat16),
            pltpu.VMEM((tiles, width, TILE), jnp.bfloat16),
            pltpu.VMEM((rows, width), jnp.bfloat16),
            pltpu.VMEM((rows, width), jnp.bfloat16),
            pltpu.VMEM((rows, width), jnp.bfloat16),
            pltpu.VMEM((tiles, rows, TILE), jnp.float32),
            pltpu.VMEM((tiles, rows, TILE), jnp.bfloat16),
            pltpu.VMEM((tiles, rows, TILE), jnp.bfloat16),
            pltpu.SemaphoreType.DMA((2,)),
            pltpu.SemaphoreType.DMA((tiles,)),
            pltpu.SemaphoreType.DMA((2,)),
            pltpu.SemaphoreType.DMA((2,)),
            pltpu.SemaphoreType.DMA((tiles,)),
            pltpu.SemaphoreType.DMA((tiles,)),
        ],
        compiler_params=pltpu.CompilerParams(
            collective_id=0, has_side_effects=True, vmem_limit_bytes=60 * 1024 * 1024
        ),
    )(
        queries.reshape(2, rows, width),
        draft_kv.reshape(2, rows, draft_kv.shape[1]),
        kv_cache,
        lengths,
        residual,
        out_proj,
        norm_gain.reshape(1, features),
    )


def expert_kernel(
    hidden,
    normed,
    gate_code,
    up,
    down,
    out,
    xa,
    xb,
    up_v,
    down_v,
    act,
    ya,
    yb,
    core_a,
    core_b,
    side_b,
    side_in_b,
    chain_a,
    chain_b,
    below_a,
    below_b,
    above_a,
    above_b,
    last_a,
    last_b,
    last_in_a,
    weight_sem,
    x_send,
    x_recv,
    core_send,
    core_recv,
    side_send,
    side_recv,
    chain_send,
    below_recv,
    above_recv,
    last_sem,
):
    ep = lax.axis_index("ep")
    tx = lax.axis_index("tp")
    z = ep // 2
    c = ep % 2
    other = 1 - c
    peer = 1 - tx
    levels, _, _, rows, width_a = xa.shape
    features = normed.shape[1]
    width_b = features - width_a
    inner = up.shape[2]
    up_copy = pltpu.make_async_copy(up.at[0], up_v, weight_sem.at[0])
    down_copy = pltpu.make_async_copy(down.at[0], down_v, weight_sem.at[1])
    up_copy.start()
    down_copy.start()
    has_up = z < levels - 1
    has_down = z > 0
    places = (
        {"ep": ep + 2},
        {"ep": ep - 2},
        {"tp": peer},
        {"ep": z * 2 + other},
    )
    conditions = (has_up, has_down, None, None)

    def when(condition, action):
        if condition is None:
            action()
        else:
            pl.when(condition)(action)

    xa[z, c, tx] = normed[:, :width_a]
    xb[z, c, tx, :, :width_b] = normed[:, width_a:]
    xb[z, c, tx, :, width_b:] = gate_code[...]
    barrier = pltpu.get_barrier_semaphore()
    for place, condition in zip(places, conditions):
        when(
            condition,
            functools.partial(
                pl.semaphore_signal, barrier, inc=1, device_id=place, device_id_type=MESH
            ),
        )
    neighbours = 2 + (z + levels - 1) // levels + (2 * levels - 2 - z) // levels
    pl.semaphore_wait(barrier, neighbours)

    pending = []

    def both(first, second):
        return first if second is None else (second if first is None else first & second)

    def start(condition, build):
        when(condition, lambda: build().start())
        pending.append((condition, build))

    def remote(source, target, send, recv, way):
        return pltpu.make_async_remote_copy(
            src_ref=source,
            dst_ref=target,
            send_sem=send,
            recv_sem=recv,
            device_id=places[way],
            device_id_type=MESH,
        )

    blocks = (xa, xb)

    def block(part, way, zb, xt):
        return remote(
            blocks[part].at[zb, c, xt],
            blocks[part].at[zb, c, xt],
            x_send.at[part, way, zb, xt],
            x_recv.at[part, zb, c, xt],
            way,
        )

    def pass_on(part, ways, zb, xt, condition=None):
        for way in ways:
            start(
                both(condition, conditions[way]),
                functools.partial(block, part, way, zb, xt),
            )

    def landed(part, zb, cb, xt):
        pltpu.make_async_remote_copy(
            src_ref=blocks[part].at[zb, cb, xt],
            dst_ref=blocks[part].at[zb, cb, xt],
            send_sem=x_send.at[part, 2, zb, xt],
            recv_sem=x_recv.at[part, zb, cb, xt],
            device_id=places[2],
            device_id_type=MESH,
        ).wait_recv()

    def phase(d):
        if d == 0:
            pass_on(0, (2, 0, 1), z, tx)
            pass_on(1, (0, 1, 2), z, tx)
            pass_on(0, (3,), z, tx)
            pass_on(1, (3,), z, tx)
            landed(0, z, c, peer)
            pass_on(0, (0, 1, 3), z, peer)
            landed(1, z, c, peer)
            pass_on(1, (3,), z, peer)
            return
        sides = ((z - d, z >= d, 0), (z + d, z + d < levels, 1))
        for part, xt in ((0, tx), (1, tx), (0, peer)):
            for zb, valid, way in sides:
                when(valid, functools.partial(landed, part, zb, c, xt))
                pass_on(part, (way, 2, 3) if part == 1 else (way, 3), zb, xt, valid)
        for zb, valid, way in sides:
            when(valid, functools.partial(landed, 1, zb, c, peer))
            pass_on(1, (3,), zb, peer, valid)

    tile = 256
    wide = 512

    def feed(zk):
        for part in (0, 1):
            for xt in (0, 1):
                landed(part, zk, other, xt)
        count = 4 * rows
        code = xb[zk, :, :, :, width_b:].reshape(count, 128).astype(jnp.float32)
        lane = lax.broadcasted_iota(jnp.int32, code.shape, 1) % 64
        gate = jnp.sum(jnp.where(lane == ep, code, 0.0), axis=1, keepdims=True)

        def rise(n, carry):
            lanes = pl.ds(pl.multiple_of(n * tile, tile), tile)
            value = jnp.dot(
                xa[zk].reshape(count, width_a),
                up_v[:width_a, lanes],
                preferred_element_type=jnp.float32,
            ) + jnp.dot(
                xb[zk, :, :, :, :width_b].reshape(count, width_b),
                up_v[width_a:, lanes],
                preferred_element_type=jnp.float32,
            )
            act[:, lanes] = (value / (1.0 + jnp.exp(-value))).astype(jnp.bfloat16)
            return carry

        lax.fori_loop(0, inner // tile, rise, 0)

        def fall(target, offset, n, carry):
            value = jnp.dot(
                act[...],
                down_v[:, pl.ds(pl.multiple_of(offset + n * wide, wide), wide)],
                preferred_element_type=jnp.float32,
            )
            target[zk, :, :, :, pl.ds(pl.multiple_of(n * wide, wide), wide)] = (
                (value * gate).astype(jnp.bfloat16).reshape(2, 2, rows, wide)
            )
            return carry

        lax.fori_loop(0, width_a // wide, functools.partial(fall, ya, 0), 0)
        lax.fori_loop(0, width_b // wide, functools.partial(fall, yb, width_a), 0)

    def core_copy(part, zk):
        source, target = ((ya, core_a), (yb, core_b))[part]
        return remote(
            source.at[zk, other],
            target.at[zk],
            core_send.at[part, zk],
            core_recv.at[part, zk],
            3,
        )

    def side_copy(zk):
        return remote(side_b.at[zk], side_in_b.at[zk], side_send.at[zk], side_recv.at[zk], 2)

    f32 = jnp.float32

    def settle(zk):
        core_copy(1, zk).wait_recv()
        side_b[zk] = (yb[zk, c, peer].astype(f32) + core_b[zk, peer].astype(f32)).astype(
            jnp.bfloat16
        )
        start(None, functools.partial(side_copy, zk))
        core_copy(0, zk).wait_recv()

    order = (z, z + 1 - 2 * (z % 2), (z + 2) % 4, 3 - z)
    for k in range(levels):
        phase(k)
        if k == 0:
            up_copy.wait()
            down_copy.wait()
        feed(order[k])
        for part in (1, 0):
            start(None, functools.partial(core_copy, part, order[k]))
        if k > 0:
            settle(order[k - 1])
    settle(order[levels - 1])

    arrivals = ((below_a, below_b, below_recv), (above_a, above_b, above_recv))

    def chain_copy(part, way, zb):
        return remote(
            (chain_a, chain_b)[part].at[zb],
            arrivals[way][part].at[zb],
            chain_send.at[part, zb],
            arrivals[way][2].at[part, zb],
            way,
        )

    def own_a(zb):
        return ya[zb, c].astype(f32) + core_a[zb].astype(f32)

    def own_b(zb):
        side_copy(zb).wait_recv()
        return (
            yb[zb, c, tx].astype(f32) + core_b[zb, tx].astype(f32) + side_in_b[zb].astype(f32)
        )

    for d in range(levels - 1, 0, -1):
        for way, zb, valid, joined in (
            (0, z + d, z + d < levels, has_down),
            (1, z - d, z >= d, has_up),
        ):

            def hop(way=way, zb=zb, joined=joined):
                chain_a[zb] = own_a(zb).astype(jnp.bfloat16)
                chain_b[zb] = own_b(zb).astype(jnp.bfloat16)

                def join():
                    for part, held in ((0, chain_a), (1, chain_b)):
                        chain_copy(part, way, zb).wait_recv()
                        held[zb] = (
                            held[zb].astype(f32) + arrivals[way][part][zb].astype(f32)
                        ).astype(jnp.bfloat16)

                pl.when(joined)(join)

            pl.when(valid)(hop)
            for part in (0, 1):
                start(valid, functools.partial(chain_copy, part, way, zb))

    last_a[...] = own_a(z)
    side = own_b(z)
    last_b[...] = side + hidden[:, width_a:].astype(f32)

    def gather_a(way):
        chain_copy(0, way, z).wait_recv()
        last_a[...] += arrivals[way][0][z].astype(f32)

    pl.when(has_down)(functools.partial(gather_a, 0))
    pl.when(has_up)(functools.partial(gather_a, 1))
    chain_a[z] = last_a[...].astype(jnp.bfloat16)

    def last_copy():
        return remote(chain_a.at[z, peer], last_in_a, last_sem.at[0], last_sem.at[1], 2)

    start(None, last_copy)

    def gather_b(way):
        chain_copy(1, way, z).wait_recv()
        last_b[...] += arrivals[way][1][z].astype(f32)

    pl.when(has_down)(functools.partial(gather_b, 0))
    pl.when(has_up)(functools.partial(gather_b, 1))
    out[:, width_a:] = last_b[...].astype(jnp.bfloat16)
    last_copy().wait_recv()
    out[:, :width_a] = (
        hidden[:, :width_a].astype(f32) + last_a[tx] + last_in_a[...].astype(f32)
    ).astype(jnp.bfloat16)
    for condition, build in pending:
        when(condition, lambda: build().wait_send())


def experts_paired(hidden, normed, gate_code, up_proj, down_proj):
    rows, features = hidden.shape
    inner = up_proj.shape[2]
    levels = lax.axis_size("ep") // 2
    width_a = 1536
    width_b = features - width_a
    vmem = pl.BlockSpec(memory_space=pltpu.VMEM)
    hbm = pl.BlockSpec(memory_space=pl.ANY)
    dma = pltpu.SemaphoreType.DMA

    def held(*shape, dtype=jnp.bfloat16):
        return pltpu.VMEM(shape, dtype)

    return pl.pallas_call(
        expert_kernel,
        out_shape=jax.ShapeDtypeStruct((rows, features), jnp.bfloat16),
        in_specs=[vmem, vmem, vmem, hbm, hbm],
        out_specs=vmem,
        scratch_shapes=[
            held(levels, 2, 2, rows, width_a),
            held(levels, 2, 2, rows, width_b + 128),
            held(features, inner),
            held(inner, features),
            held(4 * rows, inner),
            held(levels, 2, 2, rows, width_a),
            held(levels, 2, 2, rows, width_b),
            held(levels, 2, rows, width_a),
            held(levels, 2, rows, width_b),
            held(levels, rows, width_b),
            held(levels, rows, width_b),
            held(levels, 2, rows, width_a),
            held(levels, rows, width_b),
            held(levels, 2, rows, width_a),
            held(levels, rows, width_b),
            held(levels, 2, rows, width_a),
            held(levels, rows, width_b),
            held(2, rows, width_a, dtype=jnp.float32),
            held(rows, width_b, dtype=jnp.float32),
            held(rows, width_a),
            dma((2,)),
            dma((2, 4, levels, 2)),
            dma((2, levels, 2, 2)),
            dma((2, levels)),
            dma((2, levels)),
            dma((levels,)),
            dma((levels,)),
            dma((2, levels)),
            dma((2, levels)),
            dma((2, levels)),
            dma((2,)),
        ],
        compiler_params=pltpu.CompilerParams(
            collective_id=1, has_side_effects=True, vmem_limit_bytes=60 * 1024 * 1024
        ),
    )(hidden, normed, gate_code, up_proj, down_proj)


def code_gates(routes, route_gates, lost_device, spare_table):
    experts = lax.axis_size("ep")
    lost_id = lost_device[0]
    spare_id = jnp.sum(jnp.where(jnp.arange(experts) == lost_id, spare_table, 0))
    target = jnp.where(routes == lost_id, spare_id, routes)
    lane = jnp.arange(128)[None, None, :]
    gates = jnp.sum(
        jnp.where(target[:, :, None] == lane % 64, route_gates[:, :, None], 0.0), axis=1
    )
    high = lax.reduce_precision(gates, 8, 7)
    return jnp.where(lane[0] < 64, high, gates - high).astype(jnp.bfloat16)


def attend_general(queries, draft_kv, kv_cache, lengths, residual, out_proj, norm_gain):
    requests = lengths.shape[0]
    drafts = draft_kv.shape[0] // requests
    head_dim = draft_kv.shape[1] // 2
    head_count = queries.shape[1] // head_dim
    factor = 1.0 / math.sqrt(head_dim)
    query_heads = queries.reshape(requests, drafts, head_count, head_dim)
    draft_rows = draft_kv.reshape(requests, drafts, 2 * head_dim)
    draft_order = jnp.arange(drafts)
    block_rows = lax.all_gather(kv_cache, "tp", axis=0, tiled=True)
    amount = block_rows.shape[0]
    cached = block_rows.shape[1]
    key_rows = jnp.concatenate([block_rows[:, :, :head_dim], draft_rows[:, :, :head_dim]], 1)
    value_rows = jnp.concatenate([block_rows[:, :, head_dim:], draft_rows[:, :, head_dim:]], 1)
    scores = (
        jnp.einsum("rthd,rkd->rthk", query_heads, key_rows, preferred_element_type=jnp.float32)
        * factor
    )
    position = jnp.arange(cached + drafts)
    visible = jnp.where(
        position[None, None, :] < cached,
        position[None, None, :] < lengths[:, None, None],
        position[None, None, :] - cached <= draft_order[None, :, None],
    )
    visible = visible[:, :, None, :]
    peak = jnp.max(jnp.where(visible, scores, -jnp.inf), axis=-1, keepdims=True)
    weights = jnp.where(visible, jnp.exp(scores - peak), 0.0)
    totals = jnp.sum(weights, axis=-1, keepdims=True)
    mixture = (
        jnp.einsum(
            "rthk,rkd->rthd",
            weights.astype(jnp.bfloat16),
            value_rows,
            preferred_element_type=jnp.float32,
        )
        / totals
    )
    attended = mixture.astype(jnp.bfloat16).reshape(amount * drafts, head_count * head_dim)
    kept_rows = residual.shape[0]
    features = residual.shape[1]
    summed = lax.psum_scatter(
        jnp.dot(attended, out_proj, preferred_element_type=jnp.float32).astype(jnp.bfloat16),
        "tp",
        scatter_dimension=0,
        tiled=True,
    ).astype(jnp.float32)
    hidden = (residual.astype(jnp.float32) + summed).astype(jnp.bfloat16)
    widened = hidden.astype(jnp.float32)
    normed = (
        widened
        * lax.rsqrt(jnp.mean(widened * widened, axis=-1, keepdims=True) + EPSILON)
        * norm_gain
    ).astype(jnp.bfloat16)
    return hidden, normed


def shards(
    queries,
    draft_kv,
    kv_cache,
    lengths,
    residual,
    out_proj,
    norm_gain,
    up_proj,
    down_proj,
    routes,
    route_gates,
    lost_device,
    spare_table,
):
    kept_rows, features = residual.shape
    paired = lax.axis_size("tp") == 2 and kv_cache.shape[0] % 8 == 0
    attend = attend_paired if paired else attend_general
    hidden, normed = attend(
        queries, draft_kv, kv_cache, lengths, residual, out_proj, norm_gain
    )
    widened = hidden.astype(jnp.float32)
    if paired and lax.axis_size("ep") == 8 and kept_rows % 16 == 0:
        gate_code = code_gates(routes, route_gates, lost_device, spare_table)
        return experts_paired(hidden, normed, gate_code, up_proj, down_proj)
    experts = lax.axis_size("ep")
    tp_lanes = lax.axis_size("tp")
    per_row = routes.shape[1]
    capacity = min(kept_rows, (kept_rows * per_row + experts - 1) // experts)
    lost_id = lost_device[0]
    spare_id = jnp.sum(jnp.where(jnp.arange(experts) == lost_id, spare_table, 0))
    flat_routes = routes.reshape(-1)
    is_lost = flat_routes == lost_id
    lost_count = is_lost.astype(jnp.int32)
    earlier_lost = jnp.cumsum(lost_count) - lost_count
    one_hot = (flat_routes[:, None] == jnp.arange(experts)[None, :]).astype(jnp.int32)
    earlier_same = jnp.sum((jnp.cumsum(one_hot, axis=0) - one_hot) * one_hot, axis=1)
    slot_count = 2 * capacity
    target = jnp.where(is_lost, spare_id, flat_routes)
    slot_place = jnp.where(is_lost, capacity + earlier_lost, earlier_same)
    spare_up, spare_down = (up_proj, down_proj)
    slot_index = target * slot_count + slot_place
    selector = (slot_index[None, :] == jnp.arange(experts * slot_count)[:, None]).astype(
        jnp.bfloat16
    )
    repeated = jnp.repeat(normed, per_row, axis=0)
    outgoing = jnp.dot(selector, repeated, preferred_element_type=jnp.float32).astype(jnp.bfloat16)
    outgoing = outgoing.reshape(experts, slot_count, features)
    copies = jnp.broadcast_to(outgoing[:, None], (experts, tp_lanes, slot_count, features))
    copies = copies.reshape(experts * tp_lanes, slot_count, features)
    arrived = lax.all_to_all(copies, ("ep", "tp"), split_axis=0, concat_axis=0, tiled=True)
    main_part = jnp.einsum(
        "nsd,df->nsf", arrived[:, :capacity], up_proj[0], preferred_element_type=jnp.float32
    )
    spare_part = jnp.einsum(
        "nsd,df->nsf", arrived[:, capacity:], spare_up[0], preferred_element_type=jnp.float32
    )
    main_out = jnp.einsum(
        "nsf,fd->nsd",
        jax.nn.silu(main_part).astype(jnp.bfloat16),
        down_proj[0],
        preferred_element_type=jnp.float32,
    )
    spare_out = jnp.einsum(
        "nsf,fd->nsd",
        jax.nn.silu(spare_part).astype(jnp.bfloat16),
        spare_down[0],
        preferred_element_type=jnp.float32,
    )
    terms = jnp.concatenate([main_out, spare_out], axis=1).astype(jnp.bfloat16)
    returned_parts = lax.all_to_all(terms, ("ep", "tp"), split_axis=0, concat_axis=0, tiled=True)
    returned = jnp.sum(
        returned_parts.reshape(experts, tp_lanes, slot_count, features).astype(jnp.float32), axis=1
    )
    slot_grid = slot_index.reshape(kept_rows, per_row)
    combine = jnp.sum(
        jnp.where(
            slot_grid[:, :, None] == jnp.arange(experts * slot_count)[None, None, :],
            route_gates[:, :, None],
            0.0,
        ),
        axis=1,
    )
    expert_sum = jnp.dot(
        combine,
        returned.reshape(experts * slot_count, features),
        precision=lax.Precision.HIGHEST,
        preferred_element_type=jnp.float32,
    )
    return (widened + expert_sum).astype(jnp.bfloat16)


def solution(mesh):
    return jax.shard_map(
        shards,
        mesh=mesh,
        in_specs=(
            P(("grp", "ep"), "tp"),
            P(("grp", "ep"), None),
            P(("grp", "ep", "tp"), None, None),
            P(("grp", "ep")),
            P(("grp", "ep", "tp"), None),
            P("tp", None),
            P(),
            P("ep", None, "tp"),
            P("ep", "tp", None),
            P(("grp", "ep", "tp"), None),
            P(("grp", "ep", "tp"), None),
            P("grp"),
            P("grp"),
        ),
        out_specs=P(("grp", "ep", "tp"), None),
        check_vma=False,
    )
```

```python
import functools
import math

import jax
import jax.numpy as jnp
from jax import lax
from jax.experimental import pallas as pl
from jax.experimental.pallas import tpu as pltpu
from jax.sharding import PartitionSpec as P

MESH = pl.DeviceIdType.MESH
TILE = 512

EPSILON = 1e-06


def attend_block(q_ref, out_ref, kv, draft, draft_at, lengths, first, head_dim, drafts):
    requests, cached, _ = kv.shape
    heads = q_ref.shape[1] // head_dim
    factor = 1.0 / math.sqrt(head_dim)
    pair = 2 * drafts
    rows = heads * pair
    spread = q_ref[...].astype(jnp.float32)
    draft_keys = draft[draft_at, :, :head_dim]
    draft_values = draft[draft_at, :, head_dim:]
    mixed = []
    for p in range(requests // 2):
        here = jnp.concatenate(
            [
                spread[p * pair : (p + 1) * pair, h * head_dim : (h + 1) * head_dim]
                for h in range(heads)
            ],
            0,
        ).astype(jnp.bfloat16)
        keys = kv[2 * p : 2 * p + 2, :, :head_dim].reshape(2 * cached, head_dim)
        values = kv[2 * p : 2 * p + 2, :, head_dim:].reshape(2 * cached, head_dim)
        scores = (
            lax.dot_general(
                here, keys, (((1,), (1,)), ((), ())), preferred_element_type=jnp.float32
            )
            * factor
        )
        row = lax.broadcasted_iota(jnp.int32, scores.shape, 0) % pair
        column = lax.broadcasted_iota(jnp.int32, scores.shape, 1)
        upper = row >= drafts
        length = jnp.where(upper, lengths[first + 2 * p + 1] + cached, lengths[first + 2 * p])
        begin = jnp.where(upper, cached, 0)
        seen = (column >= begin) & (column < length)
        late = (
            lax.dot_general(
                here, draft_keys, (((1,), (1,)), ((), ())), preferred_element_type=jnp.float32
            )
            * factor
        )
        late_row = lax.broadcasted_iota(jnp.int32, late.shape, 0) % pair
        late_column = lax.broadcasted_iota(jnp.int32, late.shape, 1)
        late_begin = jnp.where(late_row >= drafts, drafts, 0) + p * pair
        late_seen = (late_column >= late_begin) & (late_column <= late_row + p * pair)
        scores = jnp.where(seen, scores, -jnp.inf)
        late = jnp.where(late_seen, late, -jnp.inf)
        peak = jnp.maximum(
            jnp.max(scores, axis=1, keepdims=True), jnp.max(late, axis=1, keepdims=True)
        )
        weights = jnp.exp(scores - peak)
        late_weights = jnp.exp(late - peak)
        totals = jnp.sum(weights, axis=1, keepdims=True) + jnp.sum(
            late_weights, axis=1, keepdims=True
        )
        mixture = jnp.dot(
            weights.astype(jnp.bfloat16), values, preferred_element_type=jnp.float32
        ) + jnp.dot(
            late_weights.astype(jnp.bfloat16), draft_values, preferred_element_type=jnp.float32
        )
        mixed.append(mixture / totals)
    for h in range(heads):
        out_ref[:, h * head_dim : (h + 1) * head_dim] = jnp.concatenate(
            [part[h * pair : (h + 1) * pair] for part in mixed], 0
        ).astype(jnp.bfloat16)


def attend_kernel(
    q,
    draft,
    kv,
    lengths,
    residual,
    w,
    gain,
    hidden_out,
    normed_out,
    q_own,
    q_in,
    kv_v,
    w_v,
    att_own,
    att_out,
    att_in,
    total,
    proj_out,
    proj_in,
    local_sem,
    w_sem,
    q_sem,
    att_sem,
    send_sem,
    recv_sem,
):
    me = lax.axis_index("tp")
    peer = 1 - me
    head_dim = kv.shape[2] // 2
    requests = kv.shape[0]
    drafts = q.shape[1] // requests
    tiles = w_v.shape[0]
    q_copy = pltpu.make_async_copy(q.at[me], q_own, local_sem.at[0])
    kv_copy = pltpu.make_async_copy(kv, kv_v, local_sem.at[1])
    q_copy.start()
    kv_copy.start()

    def w_copy(n):
        return pltpu.make_async_copy(
            w.at[:, pl.ds(pl.multiple_of(n * TILE, TILE), TILE)], w_v.at[n], w_sem.at[n]
        )

    for n in range(tiles):
        w_copy(n).start()
    barrier = pltpu.get_barrier_semaphore()
    pl.semaphore_signal(barrier, inc=1, device_id={"tp": peer}, device_id_type=MESH)
    pl.semaphore_wait(barrier, 1)

    def remote(source, target, send, recv):
        return pltpu.make_async_remote_copy(
            src_ref=source,
            dst_ref=target,
            send_sem=send,
            recv_sem=recv,
            device_id={"tp": peer},
            device_id_type=MESH,
        )

    ask = remote(q.at[peer], q_in, q_sem.at[0], q_sem.at[1])
    ask.start()
    q_copy.wait()
    kv_copy.wait()
    first = me * requests
    attend_block(q_own, att_own, kv_v, draft, me, lengths, first, head_dim, drafts)
    ask.wait()
    attend_block(q_in, att_out, kv_v, draft, me, lengths, first, head_dim, drafts)
    answer = remote(att_out, att_in, att_sem.at[0], att_sem.at[1])
    answer.start()

    def own_part(n, carry):
        w_copy(n).wait()
        total[n] = jnp.dot(att_own[...], w_v[n], preferred_element_type=jnp.float32)
        return carry

    lax.fori_loop(0, tiles, own_part, 0)
    answer.wait()

    def give(n):
        return remote(proj_out.at[n], proj_in.at[n], send_sem.at[n], recv_sem.at[n])

    def peer_part(n, carry):
        proj_out[n] = jnp.dot(
            att_in[...], w_v[n], preferred_element_type=jnp.float32
        ).astype(jnp.bfloat16)
        give(n).start()
        return carry

    lax.fori_loop(0, tiles, peer_part, 0)
    squares = jnp.zeros((residual.shape[0], 1), jnp.float32)
    for n in range(tiles):
        give(n).wait()
        lanes = slice(n * TILE, (n + 1) * TILE)
        hidden = (
            residual[:, lanes].astype(jnp.float32)
            + total[n]
            + proj_in[n].astype(jnp.float32)
        ).astype(jnp.bfloat16)
        hidden_out[:, lanes] = hidden
        widened = hidden.astype(jnp.float32)
        squares += jnp.sum(widened * widened, axis=1, keepdims=True)
    scale = lax.rsqrt(squares / residual.shape[1] + EPSILON)
    for n in range(tiles):
        lanes = slice(n * TILE, (n + 1) * TILE)
        normed_out[:, lanes] = (
            hidden_out[:, lanes].astype(jnp.float32) * scale * gain[lanes][None, :]
        ).astype(jnp.bfloat16)


def attend_paired(queries, draft_kv, kv_cache, lengths, residual, out_proj, norm_gain):
    rows, features = residual.shape
    width = queries.shape[1]
    tiles = features // TILE
    vmem = pl.BlockSpec(memory_space=pltpu.VMEM)
    hbm = pl.BlockSpec(memory_space=pl.ANY)
    half = jax.ShapeDtypeStruct((rows, features), jnp.bfloat16)
    return pl.pallas_call(
        attend_kernel,
        out_shape=(half, half),
        in_specs=[
            hbm,
            vmem,
            hbm,
            pl.BlockSpec(memory_space=pltpu.SMEM),
            vmem,
            hbm,
            vmem,
        ],
        out_specs=(vmem, vmem),
        scratch_shapes=[
            pltpu.VMEM((rows, width), jnp.bfloat16),
            pltpu.VMEM((rows, width), jnp.bfloat16),
            pltpu.VMEM(kv_cache.shape, jnp.bfloat16),
            pltpu.VMEM((tiles, width, TILE), jnp.bfloat16),
            pltpu.VMEM((rows, width), jnp.bfloat16),
            pltpu.VMEM((rows, width), jnp.bfloat16),
            pltpu.VMEM((rows, width), jnp.bfloat16),
            pltpu.VMEM((tiles, rows, TILE), jnp.float32),
            pltpu.VMEM((tiles, rows, TILE), jnp.bfloat16),
            pltpu.VMEM((tiles, rows, TILE), jnp.bfloat16),
            pltpu.SemaphoreType.DMA((2,)),
            pltpu.SemaphoreType.DMA((tiles,)),
            pltpu.SemaphoreType.DMA((2,)),
            pltpu.SemaphoreType.DMA((2,)),
            pltpu.SemaphoreType.DMA((tiles,)),
            pltpu.SemaphoreType.DMA((tiles,)),
        ],
        compiler_params=pltpu.CompilerParams(
            collective_id=0, has_side_effects=True, vmem_limit_bytes=60 * 1024 * 1024
        ),
    )(
        queries.reshape(2, rows, width),
        draft_kv.reshape(2, rows, draft_kv.shape[1]),
        kv_cache,
        lengths,
        residual,
        out_proj,
        norm_gain,
    )


def expert_kernel(
    hidden,
    normed,
    routes,
    route_gates,
    lost_device,
    spare_table,
    up,
    down,
    out,
    xa,
    xb,
    up_v,
    down_v,
    act,
    ya,
    yb,
    core_a,
    core_b,
    side_b,
    side_in_b,
    chain_a,
    chain_b,
    below_a,
    below_b,
    above_a,
    above_b,
    last_a,
    last_b,
    last_in_a,
    weight_sem,
    x_send,
    x_recv,
    core_send,
    core_recv,
    side_send,
    side_recv,
    chain_send,
    below_recv,
    above_recv,
    last_sem,
):
    ep = lax.axis_index("ep")
    tx = lax.axis_index("tp")
    z = ep // 2
    c = ep % 2
    other = 1 - c
    peer = 1 - tx
    levels, _, _, rows, width_a = xa.shape
    features = normed.shape[1]
    width_b = features - width_a
    inner = up.shape[2]
    up_copy = pltpu.make_async_copy(up.at[0], up_v, weight_sem.at[0])
    down_copy = pltpu.make_async_copy(down.at[0], down_v, weight_sem.at[1])
    up_copy.start()
    down_copy.start()
    has_up = z < levels - 1
    has_down = z > 0
    places = (
        {"ep": ep + 2},
        {"ep": ep - 2},
        {"tp": peer},
        {"ep": z * 2 + other},
    )
    conditions = (has_up, has_down, None, None)

    def when(condition, action):
        if condition is None:
            action()
        else:
            pl.when(condition)(action)

    xa[z, c, tx] = normed[:, :width_a]
    xb[z, c, tx, :, :width_b] = normed[:, width_a:]
    lost_id = lost_device[0]
    spare_id = spare_table[0]
    for e in range(1, spare_table.shape[0]):
        spare_id = jnp.where(lost_id == e, spare_table[e], spare_id)
    target = jnp.where(routes[...] == lost_id, spare_id, routes[...])
    wide_lane = lax.broadcasted_iota(jnp.int32, (rows, 128), 1)
    gates = jnp.zeros((rows, 128), jnp.float32)
    for k in range(routes.shape[1]):
        gates += jnp.where(
            target[:, k : k + 1] == wide_lane % 64, route_gates[:, k : k + 1], 0.0
        )
    upper = gates.astype(jnp.bfloat16)
    lower = gates - upper.astype(jnp.float32)
    xb[z, c, tx, :, width_b:] = jnp.where(
        wide_lane < 64, upper.astype(jnp.float32), lower
    ).astype(jnp.bfloat16)
    barrier = pltpu.get_barrier_semaphore()
    for place, condition in zip(places, conditions):
        when(
            condition,
            functools.partial(
                pl.semaphore_signal, barrier, inc=1, device_id=place, device_id_type=MESH
            ),
        )
    neighbours = 2 + (z + levels - 1) // levels + (2 * levels - 2 - z) // levels
    pl.semaphore_wait(barrier, neighbours)

    pending = []

    def both(first, second):
        return first if second is None else (second if first is None else first & second)

    def start(condition, build):
        when(condition, lambda: build().start())
        pending.append((condition, build))

    def remote(source, target, send, recv, way):
        return pltpu.make_async_remote_copy(
            src_ref=source,
            dst_ref=target,
            send_sem=send,
            recv_sem=recv,
            device_id=places[way],
            device_id_type=MESH,
        )

    blocks = (xa, xb)

    def block(part, way, zb, xt):
        return remote(
            blocks[part].at[zb, c, xt],
            blocks[part].at[zb, c, xt],
            x_send.at[part, way, zb, xt],
            x_recv.at[part, zb, c, xt],
            way,
        )

    def pass_on(part, ways, zb, xt, condition=None):
        for way in ways:
            start(
                both(condition, conditions[way]),
                functools.partial(block, part, way, zb, xt),
            )

    def landed(part, zb, cb, xt):
        pltpu.make_async_remote_copy(
            src_ref=blocks[part].at[zb, cb, xt],
            dst_ref=blocks[part].at[zb, cb, xt],
            send_sem=x_send.at[part, 2, zb, xt],
            recv_sem=x_recv.at[part, zb, cb, xt],
            device_id=places[2],
            device_id_type=MESH,
        ).wait_recv()

    def phase(d):
        if d == 0:
            pass_on(0, (2, 0, 1), z, tx)
            pass_on(1, (0, 1, 2), z, tx)
            pass_on(0, (3,), z, tx)
            pass_on(1, (3,), z, tx)
            landed(0, z, c, peer)
            pass_on(0, (0, 1, 3), z, peer)
            landed(1, z, c, peer)
            pass_on(1, (3,), z, peer)
            return
        sides = ((z - d, z >= d, 0), (z + d, z + d < levels, 1))
        for part, xt in ((0, tx), (1, tx), (0, peer)):
            for zb, valid, way in sides:
                when(valid, functools.partial(landed, part, zb, c, xt))
                pass_on(part, (way, 2, 3) if part == 1 else (way, 3), zb, xt, valid)
        for zb, valid, way in sides:
            when(valid, functools.partial(landed, 1, zb, c, peer))
            pass_on(1, (3,), zb, peer, valid)

    tile = 256
    wide = 512

    def feed(zk):
        for part in (0, 1):
            for xt in (0, 1):
                landed(part, zk, other, xt)
        count = 4 * rows
        code = xb[zk, :, :, :, width_b:].reshape(count, 128).astype(jnp.float32)
        lane = lax.broadcasted_iota(jnp.int32, code.shape, 1) % 64
        gate = jnp.sum(jnp.where(lane == ep, code, 0.0), axis=1, keepdims=True)

        def rise(n, carry):
            lanes = pl.ds(pl.multiple_of(n * tile, tile), tile)
            value = jnp.dot(
                xa[zk].reshape(count, width_a),
                up_v[:width_a, lanes],
                preferred_element_type=jnp.float32,
            ) + jnp.dot(
                xb[zk, :, :, :, :width_b].reshape(count, width_b),
                up_v[width_a:, lanes],
                preferred_element_type=jnp.float32,
            )
            act[:, lanes] = (value / (1.0 + jnp.exp(-value))).astype(jnp.bfloat16)
            return carry

        lax.fori_loop(0, inner // tile, rise, 0)

        def fall(target, offset, n, carry):
            value = jnp.dot(
                act[...],
                down_v[:, pl.ds(pl.multiple_of(offset + n * wide, wide), wide)],
                preferred_element_type=jnp.float32,
            )
            target[zk, :, :, :, pl.ds(pl.multiple_of(n * wide, wide), wide)] = (
                (value * gate).astype(jnp.bfloat16).reshape(2, 2, rows, wide)
            )
            return carry

        lax.fori_loop(0, width_a // wide, functools.partial(fall, ya, 0), 0)
        lax.fori_loop(0, width_b // wide, functools.partial(fall, yb, width_a), 0)

    def core_copy(part, zk):
        source, target = ((ya, core_a), (yb, core_b))[part]
        return remote(
            source.at[zk, other],
            target.at[zk],
            core_send.at[part, zk],
            core_recv.at[part, zk],
            3,
        )

    def side_copy(zk):
        return remote(side_b.at[zk], side_in_b.at[zk], side_send.at[zk], side_recv.at[zk], 2)

    f32 = jnp.float32

    def settle(zk):
        core_copy(1, zk).wait_recv()
        side_b[zk] = (yb[zk, c, peer].astype(f32) + core_b[zk, peer].astype(f32)).astype(
            jnp.bfloat16
        )
        start(None, functools.partial(side_copy, zk))
        core_copy(0, zk).wait_recv()

    arrivals = ((below_a, below_b, below_recv), (above_a, above_b, above_recv))

    def chain_copy(part, way, zb):
        return remote(
            (chain_a, chain_b)[part].at[zb],
            arrivals[way][part].at[zb],
            chain_send.at[part, zb],
            arrivals[way][2].at[part, zb],
            way,
        )

    def own_a(zb):
        return ya[zb, c].astype(f32) + core_a[zb].astype(f32)

    def own_b(zb):
        side_copy(zb).wait_recv()
        return (
            yb[zb, c, tx].astype(f32) + core_b[zb, tx].astype(f32) + side_in_b[zb].astype(f32)
        )

    def hop(way, zb, condition, joined):
        def fill():
            for part, held, own in ((0, chain_a, own_a), (1, chain_b, own_b)):
                value = own(zb)
                if joined:
                    chain_copy(part, way, zb).wait_recv()
                    value += arrivals[way][part][zb].astype(f32)
                held[zb] = value.astype(jnp.bfloat16)
                chain_copy(part, way, zb).start()

        pl.when(condition)(fill)
        for part in (0, 1):
            pending.append((condition, functools.partial(chain_copy, part, way, zb)))

    def depart(zb):
        hop(0, zb, z == 0, False)
        hop(1, zb, z == levels - 1, False)

    order = (z, z + 1 - 2 * (z % 2), (z + 2) % 4, 3 - z)
    for k in range(levels):
        phase(k)
        if k == 0:
            up_copy.wait()
            down_copy.wait()
        feed(order[k])
        for part in (1, 0):
            start(None, functools.partial(core_copy, part, order[k]))
        if k > 0:
            settle(order[k - 1])
        if k > 1:
            depart(order[k - 1])
    settle(order[levels - 1])
    depart(order[levels - 1])

    low, high = z == 1, z == levels - 2
    for way, d, condition in (
        (0, 1, low),
        (1, 1, high),
        (0, 2, low),
        (1, 2, high),
        (1, 1, low),
        (0, 1, high),
    ):
        hop(way, z + d if way == 0 else z - d, condition, True)

    last_a[...] = own_a(z)
    side = own_b(z)
    last_b[...] = side + hidden[:, width_a:].astype(f32)

    def gather_a(way):
        chain_copy(0, way, z).wait_recv()
        last_a[...] += arrivals[way][0][z].astype(f32)

    pl.when(has_down)(functools.partial(gather_a, 0))
    pl.when(has_up)(functools.partial(gather_a, 1))
    chain_a[z] = last_a[...].astype(jnp.bfloat16)

    def last_copy():
        return remote(chain_a.at[z, peer], last_in_a, last_sem.at[0], last_sem.at[1], 2)

    start(None, last_copy)

    def gather_b(way):
        chain_copy(1, way, z).wait_recv()
        last_b[...] += arrivals[way][1][z].astype(f32)

    pl.when(has_down)(functools.partial(gather_b, 0))
    pl.when(has_up)(functools.partial(gather_b, 1))
    out[:, width_a:] = last_b[...].astype(jnp.bfloat16)
    last_copy().wait_recv()
    out[:, :width_a] = (
        hidden[:, :width_a].astype(f32) + last_a[tx] + last_in_a[...].astype(f32)
    ).astype(jnp.bfloat16)
    for condition, build in pending:
        when(condition, lambda: build().wait_send())


def experts_paired(
    hidden, normed, routes, route_gates, lost_device, spare_table, up_proj, down_proj
):
    rows, features = hidden.shape
    inner = up_proj.shape[2]
    levels = lax.axis_size("ep") // 2
    width_a = 1536
    width_b = features - width_a
    vmem = pl.BlockSpec(memory_space=pltpu.VMEM)
    hbm = pl.BlockSpec(memory_space=pl.ANY)
    smem = pl.BlockSpec(memory_space=pltpu.SMEM)
    dma = pltpu.SemaphoreType.DMA

    def held(*shape, dtype=jnp.bfloat16):
        return pltpu.VMEM(shape, dtype)

    return pl.pallas_call(
        expert_kernel,
        out_shape=jax.ShapeDtypeStruct((rows, features), jnp.bfloat16),
        in_specs=[vmem, vmem, vmem, vmem, smem, smem, hbm, hbm],
        out_specs=vmem,
        scratch_shapes=[
            held(levels, 2, 2, rows, width_a),
            held(levels, 2, 2, rows, width_b + 128),
            held(features, inner),
            held(inner, features),
            held(4 * rows, inner),
            held(levels, 2, 2, rows, width_a),
            held(levels, 2, 2, rows, width_b),
            held(levels, 2, rows, width_a),
            held(levels, 2, rows, width_b),
            held(levels, rows, width_b),
            held(levels, rows, width_b),
            held(levels, 2, rows, width_a),
            held(levels, rows, width_b),
            held(levels, 2, rows, width_a),
            held(levels, rows, width_b),
            held(levels, 2, rows, width_a),
            held(levels, rows, width_b),
            held(2, rows, width_a, dtype=jnp.float32),
            held(rows, width_b, dtype=jnp.float32),
            held(rows, width_a),
            dma((2,)),
            dma((2, 4, levels, 2)),
            dma((2, levels, 2, 2)),
            dma((2, levels)),
            dma((2, levels)),
            dma((levels,)),
            dma((levels,)),
            dma((2, levels)),
            dma((2, levels)),
            dma((2, levels)),
            dma((2,)),
        ],
        compiler_params=pltpu.CompilerParams(
            collective_id=1, has_side_effects=True, vmem_limit_bytes=60 * 1024 * 1024
        ),
    )(hidden, normed, routes, route_gates, lost_device, spare_table, up_proj, down_proj)


def attend_general(queries, draft_kv, kv_cache, lengths, residual, out_proj, norm_gain):
    requests = lengths.shape[0]
    drafts = draft_kv.shape[0] // requests
    head_dim = draft_kv.shape[1] // 2
    head_count = queries.shape[1] // head_dim
    factor = 1.0 / math.sqrt(head_dim)
    query_heads = queries.reshape(requests, drafts, head_count, head_dim)
    draft_rows = draft_kv.reshape(requests, drafts, 2 * head_dim)
    draft_order = jnp.arange(drafts)
    block_rows = lax.all_gather(kv_cache, "tp", axis=0, tiled=True)
    amount = block_rows.shape[0]
    cached = block_rows.shape[1]
    key_rows = jnp.concatenate([block_rows[:, :, :head_dim], draft_rows[:, :, :head_dim]], 1)
    value_rows = jnp.concatenate([block_rows[:, :, head_dim:], draft_rows[:, :, head_dim:]], 1)
    scores = (
        jnp.einsum("rthd,rkd->rthk", query_heads, key_rows, preferred_element_type=jnp.float32)
        * factor
    )
    position = jnp.arange(cached + drafts)
    visible = jnp.where(
        position[None, None, :] < cached,
        position[None, None, :] < lengths[:, None, None],
        position[None, None, :] - cached <= draft_order[None, :, None],
    )
    visible = visible[:, :, None, :]
    peak = jnp.max(jnp.where(visible, scores, -jnp.inf), axis=-1, keepdims=True)
    weights = jnp.where(visible, jnp.exp(scores - peak), 0.0)
    totals = jnp.sum(weights, axis=-1, keepdims=True)
    mixture = (
        jnp.einsum(
            "rthk,rkd->rthd",
            weights.astype(jnp.bfloat16),
            value_rows,
            preferred_element_type=jnp.float32,
        )
        / totals
    )
    attended = mixture.astype(jnp.bfloat16).reshape(amount * drafts, head_count * head_dim)
    kept_rows = residual.shape[0]
    features = residual.shape[1]
    summed = lax.psum_scatter(
        jnp.dot(attended, out_proj, preferred_element_type=jnp.float32).astype(jnp.bfloat16),
        "tp",
        scatter_dimension=0,
        tiled=True,
    ).astype(jnp.float32)
    hidden = (residual.astype(jnp.float32) + summed).astype(jnp.bfloat16)
    widened = hidden.astype(jnp.float32)
    normed = (
        widened
        * lax.rsqrt(jnp.mean(widened * widened, axis=-1, keepdims=True) + EPSILON)
        * norm_gain
    ).astype(jnp.bfloat16)
    return hidden, normed


def shards(
    queries,
    draft_kv,
    kv_cache,
    lengths,
    residual,
    out_proj,
    norm_gain,
    up_proj,
    down_proj,
    routes,
    route_gates,
    lost_device,
    spare_table,
):
    kept_rows, features = residual.shape
    paired = lax.axis_size("tp") == 2 and kv_cache.shape[0] % 8 == 0
    attend = attend_paired if paired else attend_general
    hidden, normed = attend(
        queries, draft_kv, kv_cache, lengths, residual, out_proj, norm_gain
    )
    widened = hidden.astype(jnp.float32)
    if paired and lax.axis_size("ep") == 8 and kept_rows % 16 == 0:
        return experts_paired(
            hidden, normed, routes, route_gates, lost_device, spare_table, up_proj, down_proj
        )
    experts = lax.axis_size("ep")
    tp_lanes = lax.axis_size("tp")
    per_row = routes.shape[1]
    capacity = min(kept_rows, (kept_rows * per_row + experts - 1) // experts)
    lost_id = lost_device[0]
    spare_id = jnp.sum(jnp.where(jnp.arange(experts) == lost_id, spare_table, 0))
    flat_routes = routes.reshape(-1)
    is_lost = flat_routes == lost_id
    lost_count = is_lost.astype(jnp.int32)
    earlier_lost = jnp.cumsum(lost_count) - lost_count
    one_hot = (flat_routes[:, None] == jnp.arange(experts)[None, :]).astype(jnp.int32)
    earlier_same = jnp.sum((jnp.cumsum(one_hot, axis=0) - one_hot) * one_hot, axis=1)
    slot_count = 2 * capacity
    target = jnp.where(is_lost, spare_id, flat_routes)
    slot_place = jnp.where(is_lost, capacity + earlier_lost, earlier_same)
    spare_up, spare_down = (up_proj, down_proj)
    slot_index = target * slot_count + slot_place
    selector = (slot_index[None, :] == jnp.arange(experts * slot_count)[:, None]).astype(
        jnp.bfloat16
    )
    repeated = jnp.repeat(normed, per_row, axis=0)
    outgoing = jnp.dot(selector, repeated, preferred_element_type=jnp.float32).astype(jnp.bfloat16)
    outgoing = outgoing.reshape(experts, slot_count, features)
    copies = jnp.broadcast_to(outgoing[:, None], (experts, tp_lanes, slot_count, features))
    copies = copies.reshape(experts * tp_lanes, slot_count, features)
    arrived = lax.all_to_all(copies, ("ep", "tp"), split_axis=0, concat_axis=0, tiled=True)
    main_part = jnp.einsum(
        "nsd,df->nsf", arrived[:, :capacity], up_proj[0], preferred_element_type=jnp.float32
    )
    spare_part = jnp.einsum(
        "nsd,df->nsf", arrived[:, capacity:], spare_up[0], preferred_element_type=jnp.float32
    )
    main_out = jnp.einsum(
        "nsf,fd->nsd",
        jax.nn.silu(main_part).astype(jnp.bfloat16),
        down_proj[0],
        preferred_element_type=jnp.float32,
    )
    spare_out = jnp.einsum(
        "nsf,fd->nsd",
        jax.nn.silu(spare_part).astype(jnp.bfloat16),
        spare_down[0],
        preferred_element_type=jnp.float32,
    )
    terms = jnp.concatenate([main_out, spare_out], axis=1).astype(jnp.bfloat16)
    returned_parts = lax.all_to_all(terms, ("ep", "tp"), split_axis=0, concat_axis=0, tiled=True)
    returned = jnp.sum(
        returned_parts.reshape(experts, tp_lanes, slot_count, features).astype(jnp.float32), axis=1
    )
    slot_grid = slot_index.reshape(kept_rows, per_row)
    combine = jnp.sum(
        jnp.where(
            slot_grid[:, :, None] == jnp.arange(experts * slot_count)[None, None, :],
            route_gates[:, :, None],
            0.0,
        ),
        axis=1,
    )
    expert_sum = jnp.dot(
        combine,
        returned.reshape(experts * slot_count, features),
        precision=lax.Precision.HIGHEST,
        preferred_element_type=jnp.float32,
    )
    return (widened + expert_sum).astype(jnp.bfloat16)


def solution(mesh):
    return jax.shard_map(
        shards,
        mesh=mesh,
        in_specs=(
            P(("grp", "ep"), "tp"),
            P(("grp", "ep"), None),
            P(("grp", "ep", "tp"), None, None),
            P(("grp", "ep")),
            P(("grp", "ep", "tp"), None),
            P("tp", None),
            P(),
            P("ep", None, "tp"),
            P("ep", "tp", None),
            P(("grp", "ep", "tp"), None),
            P(("grp", "ep", "tp"), None),
            P("grp"),
            P("grp"),
        ),
        out_specs=P(("grp", "ep", "tp"), None),
        check_vma=False,
    )
```
